32 devices in a mesh: tm: 4 (over y, x), stream: 8 (over z, core).
Axes of the slice: x: 2, y: 2, z: 4, core: 2. Of those that a mesh axis runs over, the one named last changes fastest.
Arguments:
- tokens: bfloat16 [8, 512, 768], P('stream', 'tm'), may hold values from -6 to 6
- cotangent: bfloat16 [8, 512, 768], P('stream', 'tm'), may hold values from -6 to 6
- decay: float32 [8, 512, 24], P('stream', 'tm'), may hold values from 0.4 to 1, as said below
- in_w: bfloat16 [768, 3328], P('stream'), may hold values from -0.21875 to 0.21875
- out_w: bfloat16 [1536, 768], P('stream'), may hold values from -0.15625 to 0.15625
- conv_w: float32 [4, 1792], replicated, may hold values from -3 to 3
- dskip: float32 [24], replicated, may hold values from 0.5 to 2
- norm_w: float32 [1536], replicated, may hold values from 0.1 to 1.9
Outputs:
- out: bfloat16 [8, 512, 768], P('stream', 'tm')
- grad_tokens: bfloat16 [8, 512, 768], P('stream', 'tm')
- grad_out_t: float32 [768, 1536], P(('tm', 'stream'))
The draws below stay inside these ranges and needn't reach their ends.
Inputs may be any that keep to these rules, and one draw needn't show every extreme that they name: decay lies strictly between 0 and 1.
All inputs are finite; a program needn't handle non-finite values.
Results may differ from the reference program's by a relative error of at most 0.015.
Values may be sent and summed in bfloat16 or wider, within the bound.
A program may use at most 128 MiB of HBM per device.

```python
import math
import jax
import jax.numpy as jnp
from jax import lax

D = 768
INNER = 1536
HEAD_TOTAL = 24
STATE = 128
CONV = 4
TOK_DEV = 128
STAY_LENGTH = 512
STAY_COUNT = 8
PROJ = 3328
XBC = 1792


def draw_decay(key, part):
    key_frequency, key_portion, key_jaggedness, key_spike, key_level = jax.random.split(key, 5)
    rate_low = jnp.log(0.02 / STAY_LENGTH)
    rate_high = jnp.log(1.0 / 30.0)
    base_rate = jax.random.uniform(key_frequency, (STAY_COUNT, 1, HEAD_TOTAL), jnp.float32, rate_low, rate_high)
    shard_factor = jax.random.uniform(key_portion, (STAY_COUNT, STAY_LENGTH // TOK_DEV, 1, HEAD_TOTAL), jnp.float32, jnp.log(0.5), jnp.log(2.0))
    shard_factor = jnp.broadcast_to(shard_factor, (STAY_COUNT, STAY_LENGTH // TOK_DEV, TOK_DEV, HEAD_TOTAL)).reshape(STAY_COUNT, STAY_LENGTH, HEAD_TOTAL)
    roughness = jax.random.uniform(key_jaggedness, (STAY_COUNT, STAY_LENGTH, HEAD_TOTAL), jnp.float32, 0.5, 1.5)
    step_frequency = jnp.exp(base_rate + shard_factor) * roughness
    spike_events = jax.random.bernoulli(key_spike, 2.0 / STAY_LENGTH, (STAY_COUNT, STAY_LENGTH, 1))
    spike_depth = jax.random.uniform(key_level, (STAY_COUNT, STAY_LENGTH, HEAD_TOTAL), jnp.float32, 0.5, 0.8)
    return (jnp.where(spike_events, spike_depth, 1.0) * jnp.exp(-step_frequency)).astype(jnp.float32)


def levels(rng, dims, shards, smallest, top_value):
    factor_of, own = 1.0, jax.random.fold_in(rng, 6)
    for position, shards_of in shards:
        steps = jnp.exp(jax.random.uniform(jax.random.fold_in(own, position), (shards_of,), jnp.float32, smallest / len(shards), top_value / len(shards)))
        factor_of = factor_of * jnp.repeat(steps, dims[position] // shards_of).reshape([-1 if axis == position else 1 for axis in range(len(dims))])
    return factor_of


def centred(own_key, dims, width, most, cuts=(), dtype=jnp.bfloat16):
    values = width * jax.random.normal(own_key, dims, jnp.float32)
    if cuts:
        values = values * levels(own_key, dims, cuts, -0.22, 0.18)
    return jnp.clip(values, -most, most).astype(dtype)


def setup_inputs(seed: int = 0) -> dict:
    keys = jax.random.split(jax.random.key(seed), 9)
    return {
        "tokens": centred(keys[0], (STAY_COUNT, STAY_LENGTH, D), 1.0, 6.0, ((0, 8), (1, 4))),
        "cotangent": centred(keys[1], (STAY_COUNT, STAY_LENGTH, D), 1.0, 6.0, ((0, 8), (1, 4))),
        "decay": draw_decay(jax.random.fold_in(keys[8], 71), 0),
        "in_w": centred(keys[3], (D, PROJ), D ** -0.5, 0.21875, ((0, 8),)),
        "out_w": centred(keys[4], (INNER, D), INNER ** -0.5, 0.15625, ((0, 8),)),
        "conv_w": centred(keys[5], (CONV, XBC), CONV ** -0.5, 3.0, (), jnp.float32),
        "dskip": jnp.clip(jnp.exp(jax.random.uniform(keys[6], (HEAD_TOTAL,), jnp.float32, math.log(0.5), math.log(2.0))), 0.5, 2.0),
        "norm_w": jnp.clip(1.0 + 0.18 * jax.random.normal(keys[7], (INNER,), jnp.float32), 0.1, 1.9),
    }


block_len = 128
highest = lax.Precision.HIGHEST

def conv_apply(extended, conv_weight):
    conv_taps = conv_weight.shape[0]
    row_count = extended.shape[0] - conv_taps + 1
    result = jnp.zeros((row_count, extended.shape[1]), jnp.float32)
    for offset in range(conv_taps):
        result = result + conv_weight[offset] * extended[offset:offset + row_count]
    return result

def block_ssm(carry_state, x_block, b_block, c_block, decay_log):
    cumulative = jnp.cumsum(decay_log, axis=0)
    carried = jnp.exp(cumulative)[:, :, None] * jnp.einsum('tn,hpn->thp', c_block, carry_state, precision=highest)
    scores = jnp.einsum('tn,sn->ts', c_block, b_block, precision=highest)
    later_idx = lax.broadcasted_iota(jnp.int32, scores.shape, 0)
    earlier_idx = lax.broadcasted_iota(jnp.int32, scores.shape, 1)
    causal = (later_idx >= earlier_idx)[:, :, None]
    log_gap = cumulative[:, None, :] - cumulative[None, :, :]
    weight = jnp.where(causal, jnp.exp(jnp.where(causal, log_gap, 0.0)), 0.0) * scores[:, :, None]
    inside = jnp.einsum('tsh,shp->thp', weight, x_block, precision=highest)
    fade_out = jnp.exp(cumulative[-1][None, :] - cumulative)
    added = jnp.einsum('shp,sn->hpn', fade_out[:, :, None] * x_block, b_block, precision=highest)
    carry_state = jnp.exp(cumulative[-1])[:, None, None] * carry_state + added
    return (carried + inside, carry_state)

def local_scan(conv_out, decay_log, skip_gain, head_count, state_width):
    row_count = conv_out.shape[0]
    inner_width = conv_out.shape[1] - 2 * state_width
    head_dim = inner_width // head_count
    block_rows = min(block_len, row_count)
    blocks = row_count // block_rows
    x_all = conv_out[:, :inner_width].reshape(blocks, block_rows, head_count, head_dim)
    b_all = conv_out[:, inner_width:inner_width + state_width].reshape(blocks, block_rows, state_width)
    c_all = conv_out[:, inner_width + state_width:].reshape(blocks, block_rows, state_width)
    d_all = decay_log.reshape(blocks, block_rows, head_count)

    def advance(carry_state, pieces):
        outputs, carry_state = block_ssm(carry_state, pieces[0], pieces[1], pieces[2], pieces[3])
        return (carry_state, outputs)
    start_state = jnp.zeros((head_count, head_dim, state_width), jnp.float32)
    final_state, results = lax.scan(advance, start_state, (x_all, b_all, c_all, d_all))
    x_heads = conv_out[:, :inner_width].reshape(row_count, head_count, head_dim)
    outputs = results.reshape(row_count, head_count, head_dim) + skip_gain[None, :, None] * x_heads
    return (outputs.reshape(row_count, inner_width), final_state)

def gate_norm(ssm_out, gate_in, norm_gain):
    gated = ssm_out * jax.nn.silu(gate_in)
    factor = lax.rsqrt(lax.optimization_barrier(jnp.mean(gated * gated, axis=-1, keepdims=True)) + 1e-05)
    return gated * factor * norm_gain

def stay_pass(inputs, grad_out, decay_row, in_w, out_w, conv_w, dskip, norm_w):
    projected = jnp.dot(inputs, in_w, preferred_element_type=jnp.float32).astype(jnp.bfloat16)
    gate_in = projected[:, :INNER].astype(jnp.float32)
    mix_in = projected[:, INNER:].astype(jnp.float32)
    extended = jnp.concatenate([jnp.zeros((CONV - 1, XBC), jnp.float32), mix_in], axis=0)
    pre_act, conv_back = jax.vjp(lambda values: conv_apply(values, conv_w), extended)
    conv_low = jax.nn.silu(pre_act).astype(jnp.bfloat16)
    conv_out = lax.optimization_barrier(conv_low).astype(jnp.float32)
    decay_log = jnp.log(decay_row)
    ssm_out, ssm_back = jax.vjp(lambda values: local_scan(values, decay_log, dskip, HEAD_TOTAL, STATE)[0], conv_out)
    normed, norm_back = jax.vjp(lambda first, second: gate_norm(first, second, norm_w), ssm_out, gate_in)
    normed_low = normed.astype(jnp.bfloat16)
    result = jnp.dot(normed_low, out_w, preferred_element_type=jnp.float32).astype(jnp.bfloat16)
    grad_normed = jnp.dot(grad_out, out_w.T, preferred_element_type=jnp.float32)
    grad_ssm, grad_gate = norm_back(grad_normed)
    grad_conv, = ssm_back(grad_ssm)
    sigmoid_pre = jax.nn.sigmoid(pre_act)
    grad_ext, = conv_back(grad_conv * sigmoid_pre * (1.0 + pre_act * (1.0 - sigmoid_pre)))
    grad_proj = jnp.concatenate([grad_gate, grad_ext[CONV - 1:]], axis=1).astype(jnp.bfloat16)
    grad_tokens = jnp.dot(grad_proj, in_w.T, preferred_element_type=jnp.float32).astype(jnp.bfloat16)
    grad_outw = jnp.dot(grad_out.T, normed_low, preferred_element_type=jnp.float32)
    return (result, grad_tokens, grad_outw)

def reference(tokens, cotangent, decay, in_w, out_w, conv_w, dskip, norm_w):

    def per_stay(carry, items):
        result, grad_tokens, grad_outw = stay_pass(items[0], items[1], items[2], in_w, out_w, conv_w, dskip, norm_w)
        return (carry + grad_outw, (result, grad_tokens))
    start = jnp.zeros((D, INNER), jnp.float32)
    sums, stacked = lax.scan(per_stay, start, (tokens, cotangent, decay))
    grad_scale = (STAY_COUNT * STAY_LENGTH) ** (-0.5)
    return (stacked[0], stacked[1], sums * grad_scale)
```

```python
import functools

import jax
import jax.numpy as jnp
from jax import lax
from jax.experimental import pallas as pl
from jax.experimental.pallas import tpu as pltpu
from jax.sharding import PartitionSpec as P

MESH = pl.DeviceIdType.MESH
F32, BF16 = jnp.float32, jnp.bfloat16
EXACT = lax.Precision.HIGHEST


def mm(a, b):
    return lax.dot_general(a, b, (((1,), (0,)), ((), ())), preferred_element_type=F32)


def mm_nt(a, b):
    return lax.dot_general(a, b, (((1,), (1,)), ((), ())), preferred_element_type=F32)


def mm_tn(a, b):
    return lax.dot_general(a, b, (((0,), (0,)), ((), ())), preferred_element_type=F32)


def mm_exact(a, b):
    return lax.dot_general(
        a, b, (((1,), (0,)), ((), ())), preferred_element_type=F32, precision=EXACT
    )


def greet(peers):
    barrier = pltpu.get_barrier_semaphore()
    for axis, index in peers:
        pl.semaphore_signal(barrier, inc=1, device_id={axis: index}, device_id_type=MESH)
    pl.semaphore_wait(barrier, len(peers))


def others(axis, mine, count):
    return [(axis, lax.rem(mine + d, count)) for d in range(1, count)]


def gather_kernel(
    n_tm, n_stream, own_blocks,
    tok, cot, dec, win, wout,
    tok_all, cot_all, dec_all, win_all, wout_all,
    tm_send, tm_recv, in_send, in_recv, out_send, out_recv,
):
    t, s = lax.axis_index("tm"), lax.axis_index("stream")
    z, c = s // 2, s % 2
    pairs = n_stream // 2
    own_pairs = own_blocks // 2
    sibling = s + 1 - 2 * c
    greet(
        [
            ("stream", sibling),
            ("stream", lax.rem(z + 1, pairs) * 2 + c),
            ("stream", lax.rem(z + pairs - 1, pairs) * 2 + c),
        ]
        + others("tm", t, n_tm)
    )
    targets = (s + 2, s - 2, sibling)

    def in_copy(slot, way):
        return pltpu.make_async_remote_copy(
            src_ref=win_all.at[slot], dst_ref=win_all.at[slot],
            send_sem=in_send.at[way, slot], recv_sem=in_recv.at[slot],
            device_id={"stream": targets[way]}, device_id_type=MESH,
        )

    def out_copy(slot, way):
        at = slot - t * own_blocks
        return pltpu.make_async_remote_copy(
            src_ref=wout_all.at[at], dst_ref=wout_all.at[at],
            send_sem=out_send.at[way, at], recv_sem=out_recv.at[at],
            device_id={"stream": targets[way]}, device_id_type=MESH,
        )

    def held(pair):
        return (pair >= t * own_pairs) & (pair < (t + 1) * own_pairs)

    def tm_copy(kind, peer, slot):
        src, dst = ((tok, tok_all), (cot, cot_all), (dec, dec_all))[kind]
        return pltpu.make_async_remote_copy(
            src_ref=src, dst_ref=dst.at[slot],
            send_sem=tm_send.at[kind, peer], recv_sem=tm_recv.at[kind, slot],
            device_id={"tm": peer}, device_id_type=MESH,
        )

    def passes(copy, pair, fits, act):
        slot = 2 * pair + c

        @pl.when(fits & (pair <= z) & (z < pairs - 1))
        def _():
            act(copy(slot, 0))

        @pl.when(fits & (pair >= z) & (z > 0))
        def _():
            act(copy(slot, 1))

        @pl.when(fits)
        def _():
            act(copy(slot, 2))

    def start(copy):
        copy.start()

    win_all[s] = win[...]
    passes(in_copy, z, z >= 0, start)

    @pl.when(held(z))
    def _():
        wout_all[s - t * own_blocks] = wout[...]

    passes(out_copy, z, held(z), start)
    for kind in (0, 2, 1):
        for _, peer in others("tm", t, n_tm):
            tm_copy(kind, peer, t).start()
    tok_all[t] = tok[...]
    cot_all[t] = cot[...]
    dec_all[t] = dec[...]

    for j in range(1, pairs):
        for pair, inside in ((z - j, z - j >= 0), (z + j, z + j < pairs)):

            @pl.when(inside)
            def _(pair=pair):
                in_copy(2 * pair + c, 2).wait_recv()

            passes(in_copy, pair, inside, start)

            @pl.when(inside & held(pair))
            def _(pair=pair):
                out_copy(2 * pair + c, 2).wait_recv()

            passes(out_copy, pair, inside & held(pair), start)
    for pair in range(pairs):
        in_copy(2 * pair + 1 - c, 2).wait_recv()
    for j in range(own_pairs):
        out_copy(2 * (t * own_pairs + j) + 1 - c, 2).wait_recv()
    for kind in range(3):
        for _, peer in others("tm", t, n_tm):
            tm_copy(kind, peer, peer).wait_recv()
    for pair in range(pairs):
        passes(in_copy, pair, z >= 0, lambda copy: copy.wait_send())
    for pair in range(pairs):
        passes(out_copy, pair, held(pair), lambda copy: copy.wait_send())
    for kind in range(3):
        for _, peer in others("tm", t, n_tm):
            tm_copy(kind, peer, t).wait_send()


def sigmoid(v):
    return 1.0 / (1.0 + jnp.exp(-v))


def layer_kernel(
    n_tm, n_stream, inner, heads, head_dim, states, taps,
    tok, cot, dec, win, wout, par,
    out, grad_tok, grad_out_t,
    gate_s, ext_s, pre_s, x_s, b_s, c_s, g_s, f_s, el_s, ssm_s, gw_s, nb_s,
    mask_s, decay_s, start_s, fx_s, state_s,
    sums_s, osend, orecv, gsend, grecv, psend, precv, asend, arecv,
    s_send, s_recv, o_send, o_recv, g_send, g_recv, p_send, p_recv, a_send, a_recv,
):
    t, s = lax.axis_index("tm"), lax.axis_index("stream")
    blocks, rows, _ = tok.shape
    width = heads * head_dim
    model = tok.shape[2]
    all_heads = dec.shape[2]
    tm_peers = others("tm", t, n_tm)
    stream_peers = others("stream", s, n_stream)
    greet(tm_peers + stream_peers)

    def copy(src, dst, send, recv, axis, peer, at, slot):
        return pltpu.make_async_remote_copy(
            src_ref=src.at[at], dst_ref=dst.at[slot],
            send_sem=send.at[peer], recv_sem=recv.at[slot],
            device_id={axis: peer}, device_id_type=MESH,
        )

    def s_copy(peer, slot):
        return copy(sums_s, sums_s, s_send, s_recv, "tm", peer, t, slot)

    def o_copy(peer, slot):
        return copy(osend, orecv, o_send, o_recv, "tm", peer, peer, slot)

    def g_copy(peer, slot):
        return copy(gsend, grecv, g_send, g_recv, "tm", peer, peer, slot)

    def p_copy(peer, slot):
        return copy(psend, precv, p_send, p_recv, "stream", peer, peer, slot)

    def a_copy(peer, slot):
        return copy(asend, arecv, a_send, a_recv, "tm", peer, peer, slot)

    conv_w = [par[k : k + 1, :] for k in range(taps)]
    gain = par[taps : taps + 1, :width]
    skip = par[taps + 1 : taps + 2, :width]
    row_i = lax.broadcasted_iota(jnp.int32, (rows, rows), 0)
    col_i = lax.broadcasted_iota(jnp.int32, (rows, rows), 1)
    causal = row_i >= col_i
    tril = jnp.where(causal, 1.0, 0.0).astype(F32)
    pick_row = lax.broadcasted_iota(jnp.int32, (all_heads, width), 0) - t * heads
    pick_col = lax.broadcasted_iota(jnp.int32, (all_heads, width), 1)
    spread = jnp.where(
        (pick_col >= pick_row * head_dim) & (pick_col < (pick_row + 1) * head_dim), 1.0, 0.0
    ).astype(F32)
    one_row = lax.broadcasted_iota(jnp.int32, (all_heads, rows), 0) - t * heads
    one_col = lax.broadcasted_iota(jnp.int32, (all_heads, rows), 1)
    single = jnp.where(one_row == one_col, 1.0, 0.0).astype(F32)

    ext_s[0:8, :] = jnp.zeros((8, ext_s.shape[1]), F32)
    state_s[...] = jnp.zeros_like(state_s)

    def forward(q, carry):
        at = pl.multiple_of(q * rows, rows)
        here = pl.ds(at, rows)
        projected = mm(tok[q], win[...]).astype(BF16).astype(F32)
        gate = projected[:, :width]
        gate_s[here, :] = gate
        ext_s[pl.ds(pl.multiple_of(at + 8, 8), rows), :] = projected[:, width:]
        ext = ext_s[pl.ds(at, rows + 8), :]
        pre = conv_w[0] * ext[9 - taps : 9 - taps + rows]
        for k in range(1, taps):
            pre = pre + conv_w[k] * ext[9 - taps + k : 9 - taps + k + rows]
        pre_s[here, :] = pre
        conv = (pre * sigmoid(pre)).astype(BF16)
        x, b, c = conv[:, :width], conv[:, width : width + states], conv[:, width + states :]
        x_s[here, :] = x
        b_s[here, :] = b
        c_s[here, :] = c
        log_decay = jnp.log(dec[q])
        total = mm_exact(tril, mm_exact(log_decay, spread))
        across = mm_exact(tril, mm_exact(log_decay, single)).T
        last = total[rows - 1 : rows, :]
        grow = jnp.exp(total)
        fade = jnp.exp(last - total)
        g_s[here, :] = grow
        f_s[here, :] = fade
        end = jnp.exp(last)
        el_s[q] = jnp.broadcast_to(end, (8, width))
        x32 = x.astype(F32)
        faded = (fade * x32).astype(BF16)
        fx_s[here, :] = faded
        held = state_s[...]
        held_low = held.astype(BF16)
        start_s[q] = held_low
        state_s[...] = end * held + mm_tn(b, faded)
        scores = mm_nt(c, b)
        inside = []
        for h in range(heads):
            lo = h * head_dim
            gap = total[:, lo : lo + 1] - across[h : h + 1, :]
            weight = jnp.where(causal, jnp.exp(jnp.where(causal, gap, 0.0)), 0.0)
            decay_s[q * heads + h] = weight.astype(BF16)
            mix = (weight * scores).astype(BF16)
            mask_s[q * heads + h] = mix
            inside.append(mm(mix, x[:, lo : lo + head_dim]))
        ssm = jnp.concatenate(inside, axis=1) + grow * mm(c, held_low) + skip * x32
        ssm_s[here, :] = ssm
        gated = ssm * (gate * sigmoid(gate))
        weighted = mm_nt(cot[q], wout[...]) * gain
        gw_s[here, :] = weighted
        square = jnp.sum(gated * gated, axis=1, keepdims=True)
        cross = jnp.sum(weighted * gated, axis=1, keepdims=True)
        pair = jnp.where(col_i == 0, square, jnp.where(col_i == 1, cross, 0.0))
        sums_s[t, q] = pair.T[0:8, :]
        return carry

    lax.fori_loop(0, blocks, forward, 0)

    for _, peer in tm_peers:
        s_copy(peer, t).start()
    for _, peer in tm_peers:
        s_copy(peer, peer).wait_recv()

    def normed_rows(q):
        both = sums_s[0, q]
        for k in range(1, n_tm):
            both = both + sums_s[k, q]
        columns = jnp.concatenate([both, jnp.zeros((rows - 8, rows), F32)], axis=0).T
        factor = lax.rsqrt(columns[:, 0:1] * (1.0 / inner) + 1e-05)
        return factor, columns[:, 1:2]

    def outward(q, carry):
        here = pl.ds(pl.multiple_of(q * rows, rows), rows)
        factor, _ = normed_rows(q)
        gate = gate_s[here, :]
        normed = (ssm_s[here, :] * (gate * sigmoid(gate)) * factor * gain).astype(BF16)
        nb_s[here, :] = normed
        osend[q] = mm(normed, wout[...]).astype(BF16)

        @pl.when(q != t)
        def _():
            o_copy(q, t).start()

        return carry

    lax.fori_loop(0, blocks, outward, 0)

    share = model // n_stream
    part = share // n_tm
    product = mm_tn(cot[0], nb_s[0:rows, :])
    for q in range(1, blocks):
        product = product + mm_tn(cot[q], nb_s[q * rows : (q + 1) * rows, :])
    product = product.astype(BF16)
    to = lax.broadcasted_iota(jnp.int32, (model, model), 0)
    source = lax.broadcasted_iota(jnp.int32, (model, model), 1)
    owner = to // share
    within = to - owner * share
    slab = within // part
    wanted = slab * (part * n_stream) + owner * part + (within - slab * part)
    permute = jnp.where(source == wanted, 1.0, 0.0).astype(BF16)
    psend[...] = mm(permute, product).astype(BF16).reshape(n_stream, share, width)
    for _, peer in stream_peers:
        p_copy(peer, s).start()

    state_s[...] = jnp.zeros_like(state_s)

    def backward(step, carry):
        q = blocks - 1 - step
        at = pl.multiple_of(q * rows, rows)
        here = pl.ds(at, rows)
        factor, cross = normed_rows(q)
        gate = gate_s[here, :]
        ssm = ssm_s[here, :]
        sig = sigmoid(gate)
        silu = gate * sig
        gated = ssm * silu
        grad_gated = gw_s[here, :] * factor - gated * (
            factor * factor * factor * cross * (1.0 / inner)
        )
        grad_ssm = grad_gated * silu
        grad_gate = grad_gated * ssm * (sig * (1.0 + gate * (1.0 - sig)))
        x, b, c = x_s[here, :], b_s[here, :], c_s[here, :]
        low = grad_ssm.astype(BF16)
        grown = (g_s[here, :] * grad_ssm).astype(BF16)
        adjoint = state_s[...]
        adjoint_low = adjoint.astype(BF16)
        state_s[...] = el_s[q][0:1, :] * adjoint + mm_tn(c, grown)
        through = []
        gap = jnp.zeros((rows, rows), F32)
        for h in range(heads):
            lo = h * head_dim
            part_low = low[:, lo : lo + head_dim]
            through.append(mm_tn(mask_s[q * heads + h], part_low))
            gap = gap + mm_nt(part_low, x[:, lo : lo + head_dim]) * decay_s[
                q * heads + h
            ].astype(F32)
        gap = gap.astype(BF16)
        grad_x = (
            jnp.concatenate(through, axis=1)
            + f_s[here, :] * mm(b, adjoint_low)
            + skip * grad_ssm
        )
        grad_c = mm(gap, b) + mm_nt(grown, start_s[q])
        grad_b = mm_tn(gap, c) + mm_nt(fx_s[here, :], adjoint_low)
        pre = pre_s[here, :]
        sig_pre = sigmoid(pre)
        grad_pre = jnp.concatenate([grad_x, grad_b, grad_c], axis=1) * (
            sig_pre * (1.0 + pre * (1.0 - sig_pre))
        )
        ext = jnp.concatenate([grad_pre, carry], axis=0)
        grad_mix = conv_w[taps - 1] * ext[0:rows]
        for k in range(taps - 1):
            grad_mix = grad_mix + conv_w[k] * ext[taps - 1 - k : taps - 1 - k + rows]
        grad_proj = jnp.concatenate([grad_gate.astype(BF16), grad_mix.astype(BF16)], axis=1)
        gsend[q] = mm_nt(grad_proj, win[...]).astype(BF16)

        @pl.when(q != t)
        def _():
            g_copy(q, t).start()

        return grad_pre[0:8]

    lax.fori_loop(0, blocks, backward, jnp.zeros((8, width + 2 * states), F32))

    for _, peer in stream_peers:
        p_copy(peer, peer).wait_recv()
    total = psend[s].astype(F32)
    for _, peer in stream_peers:
        total = total + precv[peer].astype(F32)
    for k in range(n_tm):
        asend[k] = total[k * part : (k + 1) * part, :]
    for _, peer in tm_peers:
        a_copy(peer, t).start()
    for _, peer in tm_peers:
        o_copy(peer, peer).wait_recv()
    result = osend[t].astype(F32)
    for _, peer in tm_peers:
        result = result + orecv[peer].astype(F32)
    out[...] = result.astype(BF16)
    for _, peer in tm_peers:
        g_copy(peer, peer).wait_recv()
    result = gsend[t].astype(F32)
    for _, peer in tm_peers:
        result = result + grecv[peer].astype(F32)
    grad_tok[...] = result.astype(BF16)
    for _, peer in tm_peers:
        a_copy(peer, peer).wait_recv()
    arecv[t] = asend[t]
    scale = (n_stream * blocks * rows) ** (-0.5)
    grad_out_t[...] = (
        jnp.concatenate([arecv[k] for k in range(n_tm)], axis=1) * scale
    )
    for _, peer in tm_peers:
        s_copy(peer, t).wait_send()
        o_copy(peer, t).wait_send()
        g_copy(peer, t).wait_send()
        a_copy(peer, t).wait_send()
    for _, peer in stream_peers:
        p_copy(peer, s).wait_send()


def shards(n_tm, n_stream, tokens, cotangent, decay, in_w, out_w, conv_w, dskip, norm_w):
    t = lax.axis_index("tm")
    rows, model = tokens.shape[1:]
    all_heads = dskip.shape[0]
    inner = norm_w.shape[0]
    states = (in_w.shape[1] - 2 * inner) // 2
    taps = conv_w.shape[0]
    heads = all_heads // n_tm
    head_dim = inner // all_heads
    width = heads * head_dim
    wide = width + 2 * states
    span = width + wide

    def mine(a, axis, offset=0):
        return lax.dynamic_slice_in_dim(a, offset + t * width, width, axis)

    win = jnp.concatenate(
        [mine(in_w, 1), mine(in_w, 1, inner), in_w[:, 2 * inner :]], axis=1
    )
    tail = jnp.zeros((2 * states,), F32)
    skip = jnp.repeat(lax.dynamic_slice_in_dim(dskip, t * heads, heads), head_dim)
    par = jnp.concatenate(
        [
            jnp.concatenate([mine(conv_w, 1), conv_w[:, inner:]], axis=1),
            jnp.concatenate([mine(norm_w, 0), tail])[None],
            jnp.concatenate([skip, tail])[None],
        ]
    )
    own_blocks = width // out_w.shape[0]
    vmem = pl.BlockSpec(memory_space=pltpu.VMEM)
    dma = pltpu.SemaphoreType.DMA
    gathered = pl.pallas_call(
        functools.partial(gather_kernel, n_tm, n_stream, own_blocks),
        out_shape=[
            jax.ShapeDtypeStruct((n_tm, rows, model), BF16),
            jax.ShapeDtypeStruct((n_tm, rows, model), BF16),
            jax.ShapeDtypeStruct((n_tm, rows, all_heads), F32),
            jax.ShapeDtypeStruct((n_stream, in_w.shape[0], span), BF16),
            jax.ShapeDtypeStruct((own_blocks, out_w.shape[0], model), BF16),
        ],
        in_specs=[vmem] * 5,
        out_specs=[vmem] * 5,
        scratch_shapes=[
            dma((3, n_tm)), dma((3, n_tm)), dma((3, n_stream)), dma((n_stream,)),
            dma((3, own_blocks)), dma((own_blocks,)),
        ],
        compiler_params=pltpu.CompilerParams(
            collective_id=0, has_side_effects=True, vmem_limit_bytes=32 * 2**20
        ),
        name="gather",
    )(tokens[0], cotangent[0], decay[0], win, out_w)
    tok, cot, dec, win, wout = gathered
    win = win.reshape(model, span)
    wout = wout.reshape(width, model)
    length = n_tm * rows
    share = model // n_stream
    part = share // n_tm
    V = pltpu.VMEM
    out, grad_tok, grad_out_t = pl.pallas_call(
        functools.partial(
            layer_kernel, n_tm, n_stream, inner, heads, head_dim, states, taps
        ),
        out_shape=[
            jax.ShapeDtypeStruct((rows, model), BF16),
            jax.ShapeDtypeStruct((rows, model), BF16),
            jax.ShapeDtypeStruct((part, inner), F32),
        ],
        in_specs=[vmem] * 6,
        out_specs=[vmem] * 3,
        scratch_shapes=[
            V((length, width), F32), V((length + 8, wide), F32), V((length, wide), F32),
            V((length, width), BF16), V((length, states), BF16),
            V((length, states), BF16), V((length, width), F32), V((length, width), F32),
            V((n_tm, 8, width), F32), V((length, width), F32), V((length, width), F32),
            V((length, width), BF16), V((n_tm * heads, rows, rows), BF16),
            V((n_tm * heads, rows, rows), BF16), V((n_tm, states, width), BF16),
            V((length, width), BF16), V((states, width), F32),
            V((n_tm, n_tm, 8, rows), F32),
            V((n_tm, rows, model), BF16), V((n_tm, rows, model), BF16),
            V((n_tm, rows, model), BF16), V((n_tm, rows, model), BF16),
            V((n_stream, share, width), BF16), V((n_stream, share, width), BF16),
            V((n_tm, part, width), F32), V((n_tm, part, width), F32),
            dma((n_tm,)), dma((n_tm,)), dma((n_tm,)), dma((n_tm,)), dma((n_tm,)), dma((n_tm,)),
            dma((n_stream,)), dma((n_stream,)), dma((n_tm,)), dma((n_tm,)),
        ],
        compiler_params=pltpu.CompilerParams(
            collective_id=1, has_side_effects=True, vmem_limit_bytes=48 * 2**20
        ),
        name="layer",
    )(tok, cot, dec, win, wout, par)
    return out[None], grad_tok[None], grad_out_t


def solution(mesh):
    in_specs = (
        P("stream", "tm", None),
        P("stream", "tm", None),
        P("stream", "tm", None),
        P("stream", None),
        P("stream", None),
        P(),
        P(),
        P(),
    )
    out_specs = (P("stream", "tm", None), P("stream", "tm", None), P(("tm", "stream"), None))
    return jax.shard_map(
        functools.partial(shards, mesh.shape["tm"], mesh.shape["stream"]),
        mesh=mesh, in_specs=in_specs, out_specs=out_specs, check_vma=False,
    )
```

```python
import functools

import jax
import jax.numpy as jnp
from jax import lax
from jax.experimental import pallas as pl
from jax.experimental.pallas import tpu as pltpu
from jax.sharding import PartitionSpec as P

MESH = pl.DeviceIdType.MESH
F32, BF16 = jnp.float32, jnp.bfloat16
EXACT = lax.Precision.HIGHEST


def mm(a, b):
    return lax.dot_general(a, b, (((1,), (0,)), ((), ())), preferred_element_type=F32)


def mm_nt(a, b):
    return lax.dot_general(a, b, (((1,), (1,)), ((), ())), preferred_element_type=F32)


def mm_tn(a, b):
    return lax.dot_general(a, b, (((0,), (0,)), ((), ())), preferred_element_type=F32)


def mm_exact(a, b, over=1):
    return lax.dot_general(
        a, b, (((over,), (0,)), ((), ())), preferred_element_type=F32, precision=EXACT
    )


def greet(peers):
    barrier = pltpu.get_barrier_semaphore()
    for axis, index in peers:
        pl.semaphore_signal(barrier, inc=1, device_id={axis: index}, device_id_type=MESH)
    pl.semaphore_wait(barrier, len(peers))


def others(axis, mine, count):
    return [(axis, lax.rem(mine + d, count)) for d in range(1, count)]


def sigmoid(v):
    return 1.0 / (1.0 + jnp.exp(-v))


def layer_kernel(
    n_tm, n_stream, inner, heads, head_dim, states, taps,
    tok_in, cot_in, dec_in, win_in, wout_in, conv_in, gain_in, skip_in,
    out, grad_tok, grad_out_t,
    tok, cot, dec, win_own, win_all, wout_all, win, wout, par, permute,
    gate_s, pre_s, x_s, b_s, c_s, g_s, f_s, el_s, ssm_s, gw_s, nb_s,
    mask_s, decay_s, start_s, fx_s, state_s,
    sums_s, osend, orecv, gsend, grecv, psend, precv, asend, arecv,
    local, tm_send, tm_recv, in_send, in_recv, out_send, out_recv,
    s_send, s_recv, o_send, o_recv, g_send, g_recv, p_send, p_recv, a_send, a_recv,
):
    t, s = lax.axis_index("tm"), lax.axis_index("stream")
    z, c = s // 2, s % 2
    pairs = n_stream // 2
    blocks, rows, model = tok.shape
    width = heads * head_dim
    all_heads = dec.shape[1]
    own_blocks = wout_all.shape[0]
    own_pairs = own_blocks // 2
    sibling = s + 1 - 2 * c
    tm_peers = others("tm", t, n_tm)
    stream_peers = others("stream", s, n_stream)

    def held(pair):
        return (pair >= t * own_pairs) & (pair < (t + 1) * own_pairs)

    own_win = pltpu.make_async_copy(win_in, win_own, local.at[0])
    own_win.start()
    stays = [
        pltpu.make_async_copy(src, dst.at[t], local.at[1 + i])
        for i, (src, dst) in enumerate(((tok_in, tok), (dec_in, dec), (cot_in, cot)))
    ]
    for stay in stays:
        stay.start()
    own_wout = pltpu.make_async_copy(
        wout_in, wout_all.at[jnp.clip(s - t * own_blocks, 0, own_blocks - 1)], local.at[4]
    )

    @pl.when(held(z))
    def _():
        own_wout.start()

    for k in range(n_tm):

        @pl.when(t == k)
        def _(k=k):
            lo, hi = k * width, (k + 1) * width
            par[0:taps, 0:width] = conv_in[:, lo:hi]
            par[taps : taps + 1, 0:width] = gain_in[:, lo:hi]

    par[0:taps, width:] = conv_in[:, inner:]
    own_win.wait()
    for k in range(n_tm):

        @pl.when(t == k)
        def _(k=k):
            lo, hi = k * width, (k + 1) * width
            win_all[s, :, 0:width] = win_own[:, lo:hi]
            win_all[s, :, width : 2 * width] = win_own[:, inner + lo : inner + hi]

    win_all[s, :, 2 * width :] = win_own[:, 2 * inner :]
    greet(tm_peers + stream_peers)
    targets = (s + 2, s - 2, sibling)

    def in_copy(slot, way):
        return pltpu.make_async_remote_copy(
            src_ref=win_all.at[slot], dst_ref=win_all.at[slot],
            send_sem=in_send.at[way, slot], recv_sem=in_recv.at[slot],
            device_id={"stream": targets[way]}, device_id_type=MESH,
        )

    def out_copy(slot, way):
        at = slot - t * own_blocks
        return pltpu.make_async_remote_copy(
            src_ref=wout_all.at[at], dst_ref=wout_all.at[at],
            send_sem=out_send.at[way, at], recv_sem=out_recv.at[at],
            device_id={"stream": targets[way]}, device_id_type=MESH,
        )

    def tm_copy(kind, peer, slot):
        src, dst = ((tok_in, tok), (dec_in, dec), (cot_in, cot))[kind]
        return pltpu.make_async_remote_copy(
            src_ref=src, dst_ref=dst.at[slot],
            send_sem=tm_send.at[kind, peer], recv_sem=tm_recv.at[kind, slot],
            device_id={"tm": peer}, device_id_type=MESH,
        )

    def passes(copy, pair, fits, act):
        slot = 2 * pair + c

        @pl.when(fits & (pair <= z) & (z < pairs - 1))
        def _():
            act(copy(slot, 0))

        @pl.when(fits & (pair >= z) & (z > 0))
        def _():
            act(copy(slot, 1))

        @pl.when(fits)
        def _():
            act(copy(slot, 2))

    def start(copy):
        copy.start()

    def relay(copy, j, fits):
        for pair, inside in ((z - j, z - j >= 0), (z + j, z + j < pairs)):
            inside = inside & fits(pair)

            @pl.when(inside)
            def _(pair=pair):
                copy(2 * pair + c, 2).wait_recv()

            passes(copy, pair, inside, start)

    passes(in_copy, z, z >= 0, start)
    for kind in (1, 0):
        for _, peer in tm_peers:
            tm_copy(kind, peer, t).start()

    @pl.when(held(z))
    def _():
        own_wout.wait()

    passes(out_copy, z, held(z), start)
    for _, peer in tm_peers:
        tm_copy(2, peer, t).start()
    for stay in stays:
        stay.wait()
    share = model // n_stream
    part = share // n_tm
    to = lax.broadcasted_iota(jnp.int32, (model, model), 0)
    source = lax.broadcasted_iota(jnp.int32, (model, model), 1)
    owner = to // share
    within = to - owner * share
    slab = within // part
    wanted = slab * (part * n_stream) + owner * part + (within - slab * part)
    permute[...] = jnp.where(source == wanted, 1.0, 0.0).astype(BF16)
    conv_w = [par[k : k + 1, :] for k in range(taps)]
    gain = par[taps : taps + 1, :width]
    row_i = lax.broadcasted_iota(jnp.int32, (rows, rows), 0)
    col_i = lax.broadcasted_iota(jnp.int32, (rows, rows), 1)
    causal = row_i >= col_i
    tril = jnp.where(causal, 1.0, 0.0).astype(F32)
    pick_row = lax.broadcasted_iota(jnp.int32, (all_heads, width), 0) - t * heads
    pick_col = lax.broadcasted_iota(jnp.int32, (all_heads, width), 1)
    spread = jnp.where(
        (pick_col >= pick_row * head_dim) & (pick_col < (pick_row + 1) * head_dim), 1.0, 0.0
    ).astype(F32)
    few = (heads + 7) // 8 * 8
    one_row = lax.broadcasted_iota(jnp.int32, (few, all_heads), 0)
    one_col = lax.broadcasted_iota(jnp.int32, (few, all_heads), 1) - t * heads
    single = jnp.where((one_row == one_col) & (one_row < heads), 1.0, 0.0).astype(F32)
    triu = jnp.where(row_i <= col_i, 1.0, 0.0).astype(F32)
    skip = mm_exact(jnp.broadcast_to(skip_in[...], (8, all_heads)), spread)[0:1, :]
    wide = width + 2 * states

    def prepare(q):
        here = slice(q * rows, (q + 1) * rows)
        log_decay = jnp.log(dec[q])
        total = mm_exact(tril, mm_exact(log_decay, spread, 0))
        across = mm_exact(mm_exact(single, log_decay), triu)
        last = total[rows - 1 : rows, :]
        g_s[here, :] = jnp.exp(total)
        f_s[here, :] = jnp.exp(last - total)
        el_s[q] = jnp.broadcast_to(jnp.exp(last), (8, width))
        for h in range(heads):
            lo = h * head_dim
            gap = total[:, lo : lo + 1] - across[h : h + 1, :]
            weight = jnp.where(causal, jnp.exp(jnp.where(causal, gap, 0.0)), 0.0)
            decay_s[q * heads + h] = weight.astype(BF16)

    for _, peer in tm_peers:
        tm_copy(1, peer, peer).wait_recv()
    for j in range(1, pairs):
        if j <= blocks:
            prepare(j - 1)
        relay(in_copy, j, lambda pair: pair >= 0)
    for q in range(pairs - 1, blocks):
        prepare(q)

    def copy(src, dst, send, recv, axis, peer, at, slot):
        return pltpu.make_async_remote_copy(
            src_ref=src.at[at], dst_ref=dst.at[slot],
            send_sem=send.at[peer], recv_sem=recv.at[slot],
            device_id={axis: peer}, device_id_type=MESH,
        )

    def s_copy(peer, slot):
        return copy(sums_s, sums_s, s_send, s_recv, "tm", peer, t, slot)

    def o_copy(peer, slot):
        return copy(osend, orecv, o_send, o_recv, "tm", peer, peer, slot)

    def g_copy(peer, slot):
        return copy(gsend, grecv, g_send, g_recv, "tm", peer, peer, slot)

    def p_copy(peer, slot):
        return copy(psend, precv, p_send, p_recv, "stream", peer, peer, slot)

    def a_copy(peer, slot):
        return copy(asend, arecv, a_send, a_recv, "tm", peer, peer, slot)

    state_s[...] = jnp.zeros_like(state_s)

    for pair in range(pairs):
        in_copy(2 * pair + 1 - c, 2).wait_recv()
    height = win_all.shape[1]
    for i in range(n_stream):
        win[i * height : (i + 1) * height, :] = win_all[i]
    for _, peer in tm_peers:
        tm_copy(0, peer, peer).wait_recv()

    def forward(q, carry):
        at = pl.multiple_of(q * rows, rows)
        here = pl.ds(at, rows)
        projected = mm(tok[q], win[...]).astype(BF16).astype(F32)
        gate = projected[:, :width]
        gate_s[here, :] = gate
        mixed = projected[:, width:]
        ext = jnp.concatenate([carry, mixed], axis=0)
        pre = conv_w[0] * ext[9 - taps : 9 - taps + rows]
        for k in range(1, taps):
            pre = pre + conv_w[k] * ext[9 - taps + k : 9 - taps + k + rows]
        pre_s[here, :] = pre
        conv = (pre * sigmoid(pre)).astype(BF16)
        x, b, c = conv[:, :width], conv[:, width : width + states], conv[:, width + states :]
        x_s[here, :] = x
        b_s[here, :] = b
        c_s[here, :] = c
        grow, fade, end = g_s[here, :], f_s[here, :], el_s[q][0:1, :]
        x32 = x.astype(F32)
        faded = (fade * x32).astype(BF16)
        fx_s[here, :] = faded
        before = state_s[...]
        held_low = before.astype(BF16)
        start_s[q] = held_low
        state_s[...] = end * before + mm_tn(b, faded)
        scores = mm_nt(c, b)
        inside = []
        for h in range(heads):
            lo = h * head_dim
            weight = decay_s[q * heads + h].astype(F32)
            mix = (weight * scores).astype(BF16)
            mask_s[q * heads + h] = mix
            inside.append(mm(mix, x[:, lo : lo + head_dim]))
        ssm = jnp.concatenate(inside, axis=1) + grow * mm(c, held_low) + skip * x32
        ssm_s[here, :] = ssm

        @pl.when(q + 1 < pairs)
        def _():
            relay(out_copy, q + 1, held)

        return mixed[rows - 8 :]

    lax.fori_loop(0, blocks, forward, jnp.zeros((8, wide), F32))
    for j in range(blocks + 1, pairs):
        relay(out_copy, j, held)
    for j in range(own_pairs):
        out_copy(2 * (t * own_pairs + j) + 1 - c, 2).wait_recv()
    height = wout_all.shape[1]
    for i in range(own_blocks):
        wout[i * height : (i + 1) * height, :] = wout_all[i]
    for _, peer in tm_peers:
        tm_copy(2, peer, peer).wait_recv()

    def inward(q, carry):
        here = pl.ds(pl.multiple_of(q * rows, rows), rows)
        gate = gate_s[here, :]
        gated = ssm_s[here, :] * (gate * sigmoid(gate))
        weighted = mm_nt(cot[q], wout[...]) * gain
        gw_s[here, :] = weighted
        square = jnp.sum(gated * gated, axis=1, keepdims=True)
        cross = jnp.sum(weighted * gated, axis=1, keepdims=True)
        pair = jnp.where(col_i == 0, square, jnp.where(col_i == 1, cross, 0.0))
        sums_s[t, q] = pair.T[0:8, :]
        return carry

    lax.fori_loop(0, blocks, inward, 0)

    for _, peer in tm_peers:
        s_copy(peer, t).start()
    for _, peer in tm_peers:
        s_copy(peer, peer).wait_recv()

    def normed_rows(q):
        both = sums_s[0, q]
        for k in range(1, n_tm):
            both = both + sums_s[k, q]
        columns = jnp.concatenate([both, jnp.zeros((rows - 8, rows), F32)], axis=0).T
        factor = lax.rsqrt(columns[:, 0:1] * (1.0 / inner) + 1e-05)
        return factor, columns[:, 1:2]

    def outward(q, carry):
        here = pl.ds(pl.multiple_of(q * rows, rows), rows)
        factor, _ = normed_rows(q)
        gate = gate_s[here, :]
        normed = (ssm_s[here, :] * (gate * sigmoid(gate)) * factor * gain).astype(BF16)
        nb_s[here, :] = normed
        return carry

    lax.fori_loop(0, blocks, outward, 0)

    def result(step, carry):
        q = lax.rem(t + 1 + step, blocks)
        here = pl.ds(pl.multiple_of(q * rows, rows), rows)
        osend[q] = mm(nb_s[here, :], wout[...]).astype(BF16)

        @pl.when(q != t)
        def _():
            o_copy(q, t).start()

        return carry

    lax.fori_loop(0, blocks, result, 0)

    product = mm_tn(cot[0], nb_s[0:rows, :])
    for q in range(1, blocks):
        product = product + mm_tn(cot[q], nb_s[q * rows : (q + 1) * rows, :])
    product = product.astype(BF16)
    psend[...] = mm(permute[...], product).astype(BF16).reshape(n_stream, share, width)
    for _, peer in stream_peers:
        p_copy(peer, s).start()

    state_s[...] = jnp.zeros_like(state_s)

    def backward(step, carry):
        q = blocks - 1 - step
        at = pl.multiple_of(q * rows, rows)
        here = pl.ds(at, rows)
        factor, cross = normed_rows(q)
        gate = gate_s[here, :]
        ssm = ssm_s[here, :]
        sig = sigmoid(gate)
        silu = gate * sig
        gated = ssm * silu
        grad_gated = gw_s[here, :] * factor - gated * (
            factor * factor * factor * cross * (1.0 / inner)
        )
        grad_ssm = grad_gated * silu
        grad_gate = grad_gated * ssm * (sig * (1.0 + gate * (1.0 - sig)))
        x, b, c = x_s[here, :], b_s[here, :], c_s[here, :]
        low = grad_ssm.astype(BF16)
        grown = (g_s[here, :] * grad_ssm).astype(BF16)
        adjoint = state_s[...]
        adjoint_low = adjoint.astype(BF16)
        state_s[...] = el_s[q][0:1, :] * adjoint + mm_tn(c, grown)
        through = []
        gap = jnp.zeros((rows, rows), F32)
        for h in range(heads):
            lo = h * head_dim
            part_low = low[:, lo : lo + head_dim]
            through.append(mm_tn(mask_s[q * heads + h], part_low))
            gap = gap + mm_nt(part_low, x[:, lo : lo + head_dim]) * decay_s[
                q * heads + h
            ].astype(F32)
        gap = gap.astype(BF16)
        grad_x = (
            jnp.concatenate(through, axis=1)
            + f_s[here, :] * mm(b, adjoint_low)
            + skip * grad_ssm
        )
        grad_c = mm(gap, b) + mm_nt(grown, start_s[q])
        grad_b = mm_tn(gap, c) + mm_nt(fx_s[here, :], adjoint_low)
        pre = pre_s[here, :]
        sig_pre = sigmoid(pre)
        grad_pre = jnp.concatenate([grad_x, grad_b, grad_c], axis=1) * (
            sig_pre * (1.0 + pre * (1.0 - sig_pre))
        )
        ext = jnp.concatenate([grad_pre, carry], axis=0)
        grad_mix = conv_w[taps - 1] * ext[0:rows]
        for k in range(taps - 1):
            grad_mix = grad_mix + conv_w[k] * ext[taps - 1 - k : taps - 1 - k + rows]
        grad_proj = jnp.concatenate([grad_gate.astype(BF16), grad_mix.astype(BF16)], axis=1)
        gsend[q] = mm_nt(grad_proj, win[...]).astype(BF16)

        @pl.when(q != t)
        def _():
            g_copy(q, t).start()

        return grad_pre[0:8]

    lax.fori_loop(0, blocks, backward, jnp.zeros((8, width + 2 * states), F32))

    for _, peer in stream_peers:
        p_copy(peer, peer).wait_recv()
    total = psend[s].astype(F32)
    for _, peer in stream_peers:
        total = total + precv[peer].astype(F32)
    for k in range(n_tm):
        asend[k] = total[k * part : (k + 1) * part, :]
    for _, peer in tm_peers:
        a_copy(peer, t).start()
    for _, peer in tm_peers:
        o_copy(peer, peer).wait_recv()
    total = osend[t].astype(F32)
    for _, peer in tm_peers:
        total = total + orecv[peer].astype(F32)
    out[...] = total.astype(BF16)
    for _, peer in tm_peers:
        g_copy(peer, peer).wait_recv()
    total = gsend[t].astype(F32)
    for _, peer in tm_peers:
        total = total + grecv[peer].astype(F32)
    grad_tok[...] = total.astype(BF16)
    for _, peer in tm_peers:
        a_copy(peer, peer).wait_recv()
    arecv[t] = asend[t]
    scale = (n_stream * blocks * rows) ** (-0.5)
    grad_out_t[...] = (
        jnp.concatenate([arecv[k] for k in range(n_tm)], axis=1) * scale
    )
    for _, peer in tm_peers:
        s_copy(peer, t).wait_send()
        o_copy(peer, t).wait_send()
        g_copy(peer, t).wait_send()
        a_copy(peer, t).wait_send()
    for _, peer in stream_peers:
        p_copy(peer, s).wait_send()
    for pair in range(pairs):
        passes(in_copy, pair, z >= 0, lambda copy: copy.wait_send())
    for pair in range(pairs):
        passes(out_copy, pair, held(pair), lambda copy: copy.wait_send())
    for kind in range(3):
        for _, peer in tm_peers:
            tm_copy(kind, peer, t).wait_send()


def shards(n_tm, n_stream, tokens, cotangent, decay, in_w, out_w, conv_w, dskip, norm_w):
    rows, model = tokens.shape[1:]
    all_heads = dskip.shape[0]
    inner = norm_w.shape[0]
    states = (in_w.shape[1] - 2 * inner) // 2
    taps = conv_w.shape[0]
    heads = all_heads // n_tm
    head_dim = inner // all_heads
    width = heads * head_dim
    wide = width + 2 * states
    span = width + wide
    own_blocks = width // out_w.shape[0]
    vmem = pl.BlockSpec(memory_space=pltpu.VMEM)
    hbm = pl.BlockSpec(memory_space=pltpu.HBM)
    dma = pltpu.SemaphoreType.DMA
    length = n_tm * rows
    share = model // n_stream
    part = share // n_tm
    V = pltpu.VMEM
    out, grad_tok, grad_out_t = pl.pallas_call(
        functools.partial(
            layer_kernel, n_tm, n_stream, inner, heads, head_dim, states, taps
        ),
        out_shape=[
            jax.ShapeDtypeStruct((rows, model), BF16),
            jax.ShapeDtypeStruct((rows, model), BF16),
            jax.ShapeDtypeStruct((part, inner), F32),
        ],
        in_specs=[hbm] * 5 + [vmem] * 3,
        out_specs=[vmem] * 3,
        scratch_shapes=[
            V((n_tm, rows, model), BF16), V((n_tm, rows, model), BF16),
            V((n_tm, all_heads, rows), F32), V(in_w.shape, BF16),
            V((n_stream, in_w.shape[0], span), BF16), V((own_blocks, out_w.shape[0], model), BF16),
            V((model, span), BF16), V((width, model), BF16), V((8, wide), F32),
            V((model, model), BF16),
            V((length, width), F32), V((length, wide), F32),
            V((length, width), BF16), V((length, states), BF16),
            V((length, states), BF16), V((length, width), F32), V((length, width), F32),
            V((n_tm, 8, width), F32), V((length, width), F32), V((length, width), F32),
            V((length, width), BF16), V((n_tm * heads, rows, rows), BF16),
            V((n_tm * heads, rows, rows), BF16), V((n_tm, states, width), BF16),
            V((length, width), BF16), V((states, width), F32),
            V((n_tm, n_tm, 8, rows), F32),
            V((n_tm, rows, model), BF16), V((n_tm, rows, model), BF16),
            V((n_tm, rows, model), BF16), V((n_tm, rows, model), BF16),
            V((n_stream, share, width), BF16), V((n_stream, share, width), BF16),
            V((n_tm, part, width), F32), V((n_tm, part, width), F32),
            dma((5,)), dma((3, n_tm)), dma((3, n_tm)), dma((3, n_stream)), dma((n_stream,)),
            dma((3, own_blocks)), dma((own_blocks,)),
            dma((n_tm,)), dma((n_tm,)), dma((n_tm,)), dma((n_tm,)), dma((n_tm,)), dma((n_tm,)),
            dma((n_stream,)), dma((n_stream,)), dma((n_tm,)), dma((n_tm,)),
        ],
        compiler_params=pltpu.CompilerParams(
            collective_id=0, has_side_effects=True, vmem_limit_bytes=60 * 2**20
        ),
        name="layer",
    )(
        tokens[0], cotangent[0], decay[0].T, in_w, out_w, conv_w, norm_w[None], dskip[None]
    )
    return out[None], grad_tok[None], grad_out_t


def solution(mesh):
    in_specs = (
        P("stream", "tm", None),
        P("stream", "tm", None),
        P("stream", "tm", None),
        P("stream", None),
        P("stream", None),
        P(),
        P(),
        P(),
    )
    out_specs = (P("stream", "tm", None), P("stream", "tm", None), P(("tm", "stream"), None))
    return jax.shard_map(
        functools.partial(shards, mesh.shape["tm"], mesh.shape["stream"]),
        mesh=mesh, in_specs=in_specs, out_specs=out_specs, check_vma=False,
    )
```
